32 devices in a mesh: grp: 2 (over x), blk: 8 (over z, y), sub: 2 (over core).
Axes of the slice: x: 2, y: 2, z: 4, core: 2. Of those that a mesh axis runs over, the one named last changes fastest.
Arguments:
- spectra: bfloat16 [16, 2, 256, 2048], P('sub', None, None, ('grp', 'blk')), parts along dimension 3, may hold values from -6 to 6
- direction: int32 [2, 8], P(None, 'blk'), may hold values 0 or 1
Outputs:
- correlations: float32 [2, 16, 64, 128, 128], P(None, ('grp', 'blk'), 'sub'), parts along dimension 1
The draws below stay inside these ranges and needn't reach their ends.
There are 2 independent parts, one for each index of `grp`. The reference program is written for one: setup_inputs(seed, part) draws one part's arguments, and reference() takes and returns one part's arrays. A program takes and returns all parts, laid end to end along the dimension named above; an argument that names none is the same for every part. Nothing has to cross between parts.
Inputs may be any that keep to these rules, and one draw needn't show every extreme that they name: direction[r, b] = 1 puts block b's partner in round r at block b + r + 1, 0 at block b - r - 1, modulo 8.
All inputs are finite; a program needn't handle non-finite values.
Results may differ from the reference program's by a relative error of at most 0.011.
Values may be sent and summed in bfloat16 or wider, within the bound.
No kernel may reach another device: no remote copies, remote signals or barrier semaphores. Data moves between devices by JAX's collectives and lax.ppermute only.
A program may use at most 128 MiB of HBM per device.

```python
import math
import jax
import jax.numpy as jnp
from jax import lax

CB = 128
F = 256
LAGS = 64
ROUNDS = 2
NB = 8
C = 1024
S = 16


def touch_ends(values, rng, smallest, top_value):
    place = [jax.random.randint(jax.random.fold_in(rng, axis), (), 0, length) for axis, length in enumerate(values.shape)]
    widest = values.shape.index(max(values.shape))
    next_to = place[:widest] + [(place[widest] + 1) % values.shape[widest]] + place[widest + 1:]
    return values.at[tuple(place)].set(smallest).at[tuple(next_to)].set(top_value)


def level_of(key, dims, split, smallest, top_value):
    factor_of, own = 1.0, jax.random.fold_in(key, 6)
    for axis_at, shards_of in split:
        draws = jnp.exp(jax.random.uniform(jax.random.fold_in(own, axis_at), (shards_of,), jnp.float32, smallest / len(split), top_value / len(split)))
        factor_of = factor_of * jnp.repeat(draws, dims[axis_at] // shards_of).reshape([-1 if axis == axis_at else 1 for axis in range(len(dims))])
    return factor_of


def bell_draw(stream_key, extent, scale, bound, split=(), held_as=jnp.bfloat16):
    drawn = jax.random.normal(stream_key, extent, jnp.float32) * scale
    if len(split) > 0:
        drawn = level_of(stream_key, extent, split, -0.22, 0.18) * drawn
    return jnp.clip(drawn, min=-bound, max=bound).astype(held_as)


def setup_inputs(seed: int = 0, part: int = 0) -> dict:
    arg_keys = jax.random.split(jax.random.key(seed), 3)
    part_keys = jax.random.split(jax.random.fold_in(arg_keys[2], part), 3)
    return {
        "spectra": bell_draw(part_keys[0], (S, 2, F, C), 1.0, 6.0, ((0, 2), (3, 8))),
        "direction": touch_ends((jax.random.randint(arg_keys[1], (ROUNDS, NB), 0, 2) < 1).astype(jnp.int32), jax.random.fold_in(arg_keys[1], 1), 0, 1),
    }


def make_table(bin_count, windows, lag_count):
    lags = jnp.arange(lag_count, dtype=jnp.int32) - lag_count // 2
    bins = jnp.arange(bin_count, dtype=jnp.int32)
    period = 2 * bin_count
    phase = (bins[None, :] * ((lags[:, None] + period) % period)) % period
    angle = phase.astype(jnp.float32) * (math.pi / bin_count)
    weight = (bin_count * windows) ** -0.5
    return (jnp.stack([jnp.cos(angle), -jnp.sin(angle)], axis=-1) * weight).astype(jnp.bfloat16)


def reference(spectra, direction):
    blocks = spectra.reshape(S, 2, F, NB, CB)
    lag_table = make_table(F, S, LAGS).astype(jnp.float32)
    rounds_out = []
    for round_index in range(ROUNDS):
        def one_block(block_index):
            sign = 2 * direction[round_index, block_index] - 1
            partner_index = ((block_index + NB + sign * (round_index + 1)) % NB).astype(jnp.int32)
            local_block = lax.dynamic_index_in_dim(blocks, block_index.astype(jnp.int32), 3, keepdims=False)
            partner = lax.dynamic_index_in_dim(blocks, partner_index, 3, keepdims=False)
            swapped = jnp.stack([partner[:, 1], -partner[:, 0]], axis=1)
            operand = jnp.concatenate([partner, swapped], axis=-1)
            cross_tile = jnp.einsum("scfi,scfj->fij", local_block.astype(jnp.float32), operand.astype(jnp.float32))
            cross_tile = cross_tile.astype(jnp.bfloat16).astype(jnp.float32).reshape(F, CB, 2, CB)
            return jnp.einsum("tfk,fikj->tij", lag_table, cross_tile)
        rounds_out.append(lax.map(one_block, jnp.arange(NB, dtype=jnp.int32)))
    return jnp.stack(rounds_out, axis=0)
```

```python
import functools
import math

import jax
import jax.numpy as jnp
from jax import lax
from jax.experimental import pallas as pl
from jax.experimental.pallas import tpu as pltpu
from jax.sharding import PartitionSpec as P

LAGS = 64
ROUNDS = 2
GROUP = 8
CHANNEL_BLOCK = 32
CHUNKS = (64, 64, 64, 64)
VMEM = 56 * 2**20


def ring_shift(x, axis, by):
    size = lax.axis_size(axis)
    return lax.ppermute(x, axis, [(i, (i + by) % size) for i in range(size)])


def pair_swap(x, axis):
    size = lax.axis_size(axis)
    return lax.ppermute(x, axis, [(i, i ^ 1) for i in range(size)])


def make_table(bin_count, windows, first_lag, lag_count):
    lags = jnp.arange(lag_count, dtype=jnp.int32) + first_lag
    bins = jnp.arange(bin_count, dtype=jnp.int32)
    period = 2 * bin_count
    phase = bins[None, :] * ((lags[:, None] + period) % period) % period
    angle = phase.astype(jnp.float32) * (math.pi / bin_count)
    weight = (bin_count * windows) ** (-0.5)
    both = jnp.stack([jnp.cos(angle), -jnp.sin(angle)], axis=1) * weight
    both = both.astype(jnp.bfloat16).reshape(lag_count, 2, bin_count // GROUP, GROUP)
    return both.transpose(0, 2, 1, 3).reshape(lag_count, 2 * bin_count)


def lag_kernel(table, re_own, re_other, im_own, im_other, p0_own, p0_other, p1_own, p1_other, *rest, has_total):
    if has_total:
        total, out, cross = rest
    else:
        out, cross = rest
    rows, depth = re_own.shape
    tile = GROUP * 16
    lag_count = table.shape[0]
    bin_of_row = lax.broadcasted_iota(jnp.int32, (GROUP, tile), 0)
    bin_of_lane = lax.broadcasted_iota(jnp.int32, (GROUP, tile), 1) // (tile // GROUP)
    same_bin = bin_of_row == bin_of_lane

    def spread(ref, i, lanes):
        return jnp.where(same_bin, jnp.broadcast_to(ref[i : i + 1, lanes], (GROUP, tile)), 0.0)

    for g in range(depth // tile):
        lanes = slice(g * tile, (g + 1) * tile)
        pieces = []
        for i in range(rows):
            own = jnp.concatenate([spread(re_own, i, lanes), spread(im_own, i, lanes)], axis=0)
            other = jnp.concatenate([spread(re_other, i, lanes), spread(im_other, i, lanes)], axis=0)
            pieces.append(jnp.concatenate([own, other], axis=1).astype(jnp.bfloat16))
        left = jnp.concatenate(pieces, axis=0)
        right = jnp.concatenate(
            [
                jnp.concatenate([p0_own[lanes, :], p1_own[lanes, :]], axis=1),
                jnp.concatenate([p0_other[lanes, :], p1_other[lanes, :]], axis=1),
            ],
            axis=0,
        )
        part = jnp.dot(left, right, preferred_element_type=jnp.float32).astype(jnp.bfloat16)
        cross[:, g * 2 * GROUP : (g + 1) * 2 * GROUP, :] = part.reshape(rows, 2 * GROUP, part.shape[-1])

    for first in range(0, rows, 8):
        lagged = [
            jnp.dot(table[...], cross[i], preferred_element_type=jnp.float32) for i in range(first, first + 8)
        ]
        for r in range(ROUNDS):
            width = p0_own.shape[1]
            stacked = jnp.stack([x[:, r * width : (r + 1) * width] for x in lagged], axis=0)
            tile_out = jnp.swapaxes(stacked, 0, 1)
            if has_total:
                tile_out = tile_out + total[r, :, first : first + 8, :]
            out[r, :, first : first + 8, :] = tile_out


def add_lags(table, local, partners, total):
    lag_count, cross_depth = table.shape
    channels, depth = local[0].shape
    width = partners[0].shape[1]
    block = CHANNEL_BLOCK
    whole = lambda b: (0, 0)
    part = lambda b: (b, 0)
    out_spec = pl.BlockSpec((ROUNDS, lag_count, block, width), lambda b: (0, 0, b, 0))
    in_specs = [pl.BlockSpec((lag_count, cross_depth), whole)]
    in_specs += [pl.BlockSpec((block, depth), part) for _ in local]
    in_specs += [pl.BlockSpec((depth, width), whole) for _ in partners]
    operands = [table, *local, *partners]
    aliases = {}
    if total is not None:
        in_specs.append(out_spec)
        aliases = {len(operands): 0}
        operands.append(total)
    out_shape = jax.ShapeDtypeStruct((ROUNDS, lag_count, channels, width), jnp.float32)
    return pl.pallas_call(
        functools.partial(lag_kernel, has_total=total is not None),
        grid=(channels // block,),
        in_specs=in_specs,
        out_specs=out_spec,
        out_shape=out_shape,
        input_output_aliases=aliases,
        scratch_shapes=[pltpu.VMEM((block, cross_depth, ROUNDS * width), jnp.bfloat16)],
        compiler_params=pltpu.CompilerParams(vmem_limit_bytes=VMEM),
        cost_estimate=pl.CostEstimate(
            flops=2 * channels * cross_depth * 256 * 256, bytes_accessed=8 * 2**20, transcendentals=0
        ),
    )(*operands)


def bins_first_kernel(x, *outs, sizes, first):
    for out, size in zip(outs, sizes):
        for low in range(0, size, 16):
            at = slice(first + low, first + low + 16)
            slabs = [x[s, c, at, :].astype(jnp.float32) for c in range(2) for s in range(x.shape[0])]
            turned = jnp.swapaxes(jnp.stack(slabs, axis=0), 0, 1)
            rows = turned.reshape(16 * len(slabs), x.shape[3]).astype(out.dtype)
            out[low * len(slabs) : (low + 16) * len(slabs), :] = rows
        first += size


def bins_first(x, first, sizes):
    windows, parts, bins, channels = x.shape
    read = bins if first else sum(sizes)
    return pl.pallas_call(
        functools.partial(bins_first_kernel, sizes=sizes, first=first),
        grid=(1,),
        in_specs=[pl.BlockSpec((windows, parts, read, channels), lambda b: (0, 0, 0, 0))],
        out_specs=[pl.BlockSpec((size * parts * windows, channels), lambda b: (0, 0)) for size in sizes],
        out_shape=[jax.ShapeDtypeStruct((size * parts * windows, channels), x.dtype) for size in sizes],
        compiler_params=pltpu.CompilerParams(vmem_limit_bytes=VMEM),
    )(x)


def channels_first_kernel(*refs, count):
    ins, outs = refs[: 2 * count], refs[2 * count :]
    for n in range(2 * count):
        rows, channels = ins[n].shape
        for low in range(0, rows, 128):
            tile = ins[n][low : low + 128, :].astype(jnp.float32).T
            lane = lax.broadcasted_iota(jnp.int32, tile.shape, 1)
            real_lane = lane % 16 < 8
            outs[n][:, low : low + 128] = tile
            swapped = jnp.where(real_lane, -pltpu.roll(tile, 128 - 8, 1), pltpu.roll(tile, 8, 1))
            outs[2 * count + n][:, low : low + 128] = swapped


def channels_first(own, other):
    shapes = [jax.ShapeDtypeStruct(x.shape[::-1], jnp.float32) for x in (*own, *other)]
    outs = pl.pallas_call(
        functools.partial(channels_first_kernel, count=len(own)),
        out_shape=shapes + shapes,
        compiler_params=pltpu.CompilerParams(vmem_limit_bytes=VMEM),
    )(*own, *other)
    count = len(own)
    return [[outs[n], outs[count + n], outs[2 * count + n], outs[3 * count + n]] for n in range(count)]


def choose_kernel(picks, mine, behind, ahead, *rest):
    far, near = rest[-2:]
    far[...] = jnp.where(picks[0] == 1, ahead[...], behind[...])
    near[...] = jnp.where(picks[1] == 1, mine[...], jnp.where(picks[2] == 1, behind[...], ahead[...]))


def choose(picks, mine, behind, ahead, after):
    vmem = pl.BlockSpec(memory_space=pltpu.VMEM)
    return pl.pallas_call(
        choose_kernel,
        in_specs=[pl.BlockSpec(memory_space=pltpu.SMEM), vmem, vmem, vmem]
        + [pl.BlockSpec(memory_space=pl.ANY)] * len(after),
        out_specs=[vmem, vmem],
        out_shape=[jax.ShapeDtypeStruct(mine.shape, mine.dtype)] * 2,
        compiler_params=pltpu.CompilerParams(vmem_limit_bytes=VMEM),
    )(picks, mine, behind, ahead, *after)


def per_device(spectra, direction):
    windows, _, bin_count, channels = spectra.shape
    cores = lax.axis_size("sub")
    lag_count = LAGS // cores
    odd = lax.axis_index("blk") % 2
    near_of_pair = pair_swap(direction[0], "blk")[0]
    picks = jnp.stack([direction[1, 0], jnp.where(odd == 1, near_of_pair, 1 - near_of_pair), odd])

    table = make_table(bin_count, windows * cores, lax.axis_index("sub") * lag_count - LAGS // 2, lag_count)

    mine = bins_first(spectra, 0, CHUNKS[:1]) + bins_first(spectra, CHUNKS[0], CHUNKS[1:])
    behind = [ring_shift(x, "blk", 2) for x in mine]
    ahead = [ring_shift(x, "blk", -2) for x in mine]
    other = [ring_shift(x, "sub", 1) for x in mine]
    local = channels_first(mine, other)

    totals = [None]
    first = 0
    for n, size in enumerate(CHUNKS):
        after = [totals[n - 1]] if n >= 2 else []
        far_own, passed_on = choose(picks, mine[n], behind[n], ahead[n], after)
        near_own = pair_swap(passed_on, "blk")
        far_other = ring_shift(far_own, "sub", 1)
        near_other = ring_shift(near_own, "sub", 1)
        table_part = table[:, 2 * first : 2 * (first + size)]
        totals.append(add_lags(table_part, local[n], [near_own, near_other, far_own, far_other], totals[-1]))
        first += size
    return totals[-1][:, None]


def solution(mesh):
    return jax.shard_map(
        per_device,
        mesh=mesh,
        in_specs=(P("sub", None, None, ("grp", "blk")), P(None, "blk")),
        out_specs=P(None, ("grp", "blk"), "sub", None, None),
        check_vma=False,
    )
```

```python
import functools
import math

import jax
import jax.numpy as jnp
from jax import lax
from jax.experimental import pallas as pl
from jax.experimental.pallas import tpu as pltpu
from jax.sharding import PartitionSpec as P

LAGS = 64
ROUNDS = 2
GROUP = 8
CHANNEL_BLOCK = 32
CHUNKS = (64, 64, 64, 64)
VMEM = 32 * 2**20
AFTER = {2: 0, 3: 1}
GATE = {}
COST = pl.CostEstimate(flops=0, bytes_accessed=0, transcendentals=0)


def ring_shift(x, axis, by):
    size = lax.axis_size(axis)
    return lax.ppermute(x, axis, [(i, (i + by) % size) for i in range(size)])


def pair_swap(x, axis):
    size = lax.axis_size(axis)
    return lax.ppermute(x, axis, [(i, i ^ 1) for i in range(size)])


def make_table(bin_count, windows, lag_count):
    lags = jnp.arange(lag_count, dtype=jnp.int32) - lag_count // 2
    bins = jnp.arange(bin_count, dtype=jnp.int32)
    period = 2 * bin_count
    phase = bins[None, :] * ((lags[:, None] + period) % period) % period
    angle = phase.astype(jnp.float32) * (math.pi / bin_count)
    weight = (bin_count * windows) ** (-0.5)
    both = jnp.stack([jnp.cos(angle), -jnp.sin(angle)], axis=1) * weight
    both = both.astype(jnp.bfloat16).reshape(lag_count, 2, bin_count // GROUP, GROUP)
    return both.transpose(0, 2, 1, 3).reshape(lag_count, 2 * bin_count)


def lag_kernel(*refs, first, has_total, last):
    table, re_own, re_other, im_own, im_other, p0_own, p0_other, p1_own, p1_other = refs[:9]
    total = refs[9] if has_total else None
    out, cross = refs[9 + has_total : 11 + has_total]
    rows = CHANNEL_BLOCK
    channels, depth = re_own.shape
    width = p0_own.shape[1]
    tile = GROUP * 16
    lag_count = out.shape[1]
    mine = pl.ds(pl.multiple_of(lax.axis_index("sub") * lag_count, lag_count), lag_count)
    weights = table[mine, 2 * first : 2 * (first + depth // 16)]
    bin_of_row = lax.broadcasted_iota(jnp.int32, (GROUP, tile), 0)
    bin_of_lane = lax.broadcasted_iota(jnp.int32, (GROUP, tile), 1) // (tile // GROUP)
    same_bin = bin_of_row == bin_of_lane

    def spread(ref, i, lanes):
        return jnp.where(same_bin, jnp.broadcast_to(ref[i : i + 1, lanes], (GROUP, tile)), 0.0)

    def block(b):
        start = pl.multiple_of(b * rows, rows)
        here = [ref.at[pl.ds(start, rows), :] for ref in (re_own, im_own, re_other, im_other)]
        for g in range(depth // tile):
            lanes = slice(g * tile, (g + 1) * tile)
            pieces = []
            for i in range(rows):
                own = jnp.concatenate([spread(here[0], i, lanes), spread(here[1], i, lanes)], axis=0)
                other = jnp.concatenate([spread(here[2], i, lanes), spread(here[3], i, lanes)], axis=0)
                pieces.append(jnp.concatenate([own, other], axis=1).astype(jnp.bfloat16))
            left = jnp.concatenate(pieces, axis=0)
            right = jnp.concatenate(
                [
                    jnp.concatenate([p0_own[lanes, :], p1_own[lanes, :]], axis=1),
                    jnp.concatenate([p0_other[lanes, :], p1_other[lanes, :]], axis=1),
                ],
                axis=0,
            )
            part = jnp.dot(left, right, preferred_element_type=jnp.float32).astype(jnp.bfloat16)
            cross[:, g * 2 * GROUP : (g + 1) * 2 * GROUP, :] = part.reshape(rows, 2 * GROUP, part.shape[-1])

        for low in range(0, rows, 8):
            lagged = [jnp.dot(weights, cross[i], preferred_element_type=jnp.float32) for i in range(low, low + 8)]
            at = pl.ds(pl.multiple_of(start + low, 8), 8)
            for r in range(ROUNDS):
                stacked = jnp.stack([x[:, r * width : (r + 1) * width] for x in lagged], axis=0)
                tile_out = jnp.swapaxes(stacked, 0, 1)
                if has_total:
                    tile_out = tile_out + total[r, :, at, :]
                if last:
                    stage[b, r, :, low : low + 8, :] = tile_out
                else:
                    out[r, :, at, :] = tile_out

    if last:
        stage, sems = refs[11 + has_total :]

        def store(b):
            at = pl.ds(pl.multiple_of(b * rows, rows), rows)
            return pltpu.make_async_copy(stage.at[b], out.at[:, :, at, :], sems.at[b])

        @pl.loop(0, channels // rows)
        def _(b):
            block(b)
            store(b).start()

        for b in range(channels // rows):
            store(b).wait()
    else:

        @pl.loop(0, channels // rows)
        def _(b):
            block(b)


def add_lags(table, first, local, partners, total, last):
    channels, depth = local[0].shape
    lag_count = table.shape[0] // lax.axis_size("sub")
    cross_depth = depth // 8
    width = partners[0].shape[1]
    block = CHANNEL_BLOCK
    vmem = pl.BlockSpec(memory_space=pltpu.VMEM)
    operands = [table, *local, *partners]
    aliases = {}
    if total is not None:
        if not last:
            aliases = {len(operands): 0}
        operands.append(total)
    shape = (ROUNDS, lag_count, channels, width)
    scratch = [pltpu.VMEM((block, cross_depth, ROUNDS * width), jnp.bfloat16)]
    if last:
        blocks = channels // block
        scratch += [pltpu.VMEM((blocks, ROUNDS, lag_count, block, width), jnp.float32), pltpu.SemaphoreType.DMA((blocks,))]
    return pl.pallas_call(
        functools.partial(lag_kernel, first=first, has_total=total is not None, last=last),
        in_specs=[vmem] * len(operands),
        out_specs=pl.BlockSpec(memory_space=pl.ANY) if last else vmem,
        out_shape=jax.ShapeDtypeStruct(shape, jnp.float32) if last else pltpu.VMEM(shape, jnp.float32),
        input_output_aliases=aliases,
        scratch_shapes=scratch,
        compiler_params=pltpu.CompilerParams(vmem_limit_bytes=VMEM),
        cost_estimate=COST,
    )(*operands)


def bins_first_kernel(x, *outs, sizes, first):
    for out, size in zip(outs, sizes):
        if size == x.shape[2] and first:
            first = 0
        for low in range(0, size, 16):
            at = slice(first + low, first + low + 16)
            slabs = [x[s, c, at, :].astype(jnp.float32) for c in range(2) for s in range(x.shape[0])]
            turned = jnp.swapaxes(jnp.stack(slabs, axis=0), 0, 1)
            rows = turned.reshape(16 * len(slabs), x.shape[3]).astype(out.dtype)
            out[low * len(slabs) : (low + 16) * len(slabs), :] = rows
        first += size


def bins_first(x, first, sizes):
    windows, parts, bins, channels = x.shape
    read = bins if first else sum(sizes)
    return pl.pallas_call(
        functools.partial(bins_first_kernel, sizes=sizes, first=first),
        grid=(1,),
        in_specs=[pl.BlockSpec((windows, parts, read, channels), lambda b: (0, 0, 0, 0))],
        out_specs=[pl.BlockSpec((size * parts * windows, channels), lambda b: (0, 0)) for size in sizes],
        out_shape=[jax.ShapeDtypeStruct((size * parts * windows, channels), x.dtype) for size in sizes],
        compiler_params=pltpu.CompilerParams(vmem_limit_bytes=VMEM),
        cost_estimate=COST,
    )(x)


def channels_first_kernel(own, other, *outs):
    quarter = len(outs) // 4
    for k, ref in enumerate((own, other)):
        first = 0
        for n in range(quarter):
            plain, turned = outs[4 * n + k], outs[4 * n + 2 + k]
            depth = plain.shape[1]
            for low in range(0, depth, 128):
                tile = ref[first + low : first + low + 128, :].astype(jnp.float32).T
                real_lane = lax.broadcasted_iota(jnp.int32, tile.shape, 1) % 16 < 8
                plain[:, low : low + 128] = tile
                swapped = jnp.where(real_lane, -pltpu.roll(tile, 128 - 8, 1), pltpu.roll(tile, 8, 1))
                turned[:, low : low + 128] = swapped
            first += depth


def channels_first(own, other, depths):
    outs = pl.pallas_call(
        channels_first_kernel,
        out_shape=[pltpu.VMEM((own.shape[1], depth), jnp.float32) for depth in depths for _ in range(4)],
        in_specs=[pl.BlockSpec(memory_space=pltpu.VMEM)] * 2,
        out_specs=[pl.BlockSpec(memory_space=pltpu.VMEM)] * (4 * len(depths)),
        compiler_params=pltpu.CompilerParams(vmem_limit_bytes=VMEM),
        cost_estimate=COST,
    )(own, other)
    return [outs[4 * n : 4 * n + 4] for n in range(len(depths))]


def choose_kernel(direction, of_pair, mine, behind, ahead, *rest):
    far, near, held, sems = rest[-4:]
    odd = lax.axis_index("blk") % 2

    def fetch(source, n):
        return pltpu.make_async_copy(source, held.at[n], sems.at[n])

    pl.when(direction[1, 0] == 1)(lambda: fetch(ahead, 0).start())
    pl.when(direction[1, 0] != 1)(lambda: fetch(behind, 0).start())
    pl.when(of_pair[0] == odd)(lambda: fetch(mine, 1).start())
    pl.when((of_pair[0] != odd) & (odd == 1))(lambda: fetch(behind, 1).start())
    pl.when((of_pair[0] != odd) & (odd == 0))(lambda: fetch(ahead, 1).start())
    for n, out in enumerate((far, near)):
        fetch(mine, n).wait()
        pltpu.make_async_copy(held.at[n], out, sems.at[n]).start()
    for n, out in enumerate((far, near)):
        pltpu.make_async_copy(held.at[n], out, sems.at[n]).wait()


def choose(direction, of_pair, mine, behind, ahead, after):
    smem = pl.BlockSpec(memory_space=pltpu.SMEM)
    hbm = pl.BlockSpec(memory_space=pl.ANY)
    return pl.pallas_call(
        choose_kernel,
        in_specs=[smem, smem] + [hbm] * (3 + len(after)),
        out_specs=[hbm, hbm],
        out_shape=[jax.ShapeDtypeStruct(mine.shape, mine.dtype)] * 2,
        scratch_shapes=[pltpu.VMEM((2, *mine.shape), mine.dtype), pltpu.SemaphoreType.DMA((2,))],
        compiler_params=pltpu.CompilerParams(vmem_limit_bytes=VMEM),
        cost_estimate=COST,
    )(direction, of_pair, mine, behind, ahead, *after)


def per_device(spectra, direction):
    windows, _, bin_count, channels = spectra.shape
    with jax.named_scope("direction_of_pair"):
        of_pair = pair_swap(direction[0], "blk")
    table = make_table(bin_count, windows * lax.axis_size("sub"), LAGS)

    mine = bins_first(spectra, 0, CHUNKS[:1])
    *later, whole = bins_first(spectra, CHUNKS[0], (*CHUNKS[1:], bin_count))
    mine = [*mine, *later]
    behind, ahead = [], []
    for n, x in enumerate(mine):
        with jax.named_scope(f"two_behind_{n}"):
            behind.append(ring_shift(x, "blk", 2))
        with jax.named_scope(f"two_ahead_{n}"):
            ahead.append(ring_shift(x, "blk", -2))
    with jax.named_scope("my_other_half"):
        other = ring_shift(whole, "sub", 1)
    local = channels_first(whole, other, [size * whole.shape[0] // bin_count for size in CHUNKS])

    totals = [None]
    first = 0
    for n, size in enumerate(CHUNKS):
        after = [totals[AFTER[n] + 1]] if n in AFTER else []
        if n == 0:
            after = [local[0][0], table]
        far_own, passed_on = choose(direction, of_pair, mine[n], behind[n], ahead[n], after)
        with jax.named_scope(f"near_{n}"):
            near_own = pair_swap(passed_on, "blk")
        with jax.named_scope(f"far_other_half_{n}"):
            far_other = ring_shift(far_own, "sub", 1)
        if n in GATE:
            near_own, _ = lax.optimization_barrier((near_own, totals[GATE[n] + 1]))
        with jax.named_scope(f"near_other_half_{n}"):
            near_other = ring_shift(near_own, "sub", 1)
        totals.append(add_lags(table, first, local[n], [near_own, near_other, far_own, far_other], totals[-1], n == len(CHUNKS) - 1))
        first += size
    return totals[-1][:, None]


def solution(mesh):
    return jax.shard_map(
        per_device,
        mesh=mesh,
        in_specs=(P("sub", None, None, ("grp", "blk")), P(None, "blk")),
        out_specs=P(None, ("grp", "blk"), "sub", None, None),
        check_vma=False,
    )
```

```python
import functools
import math

import jax
import jax.numpy as jnp
from jax import lax
from jax.experimental import pallas as pl
from jax.experimental.pallas import tpu as pltpu
from jax.sharding import PartitionSpec as P

LAGS = 64
ROUNDS = 2
GROUP = 8
CHANNEL_BLOCK = 32
UNROLL = 2
CHUNKS = (64, 64, 64, 64)
VMEM = 20 * 2**20
AFTER = {3: 0}
GATE = {3: 2}
NEAR_GATE = {}
SPLIT = False
EXPAND = {}
GATE_FAR = False
LAG_FLOPS = 3e9
COST = pl.CostEstimate(flops=0, bytes_accessed=0, transcendentals=0)


def ring_shift(x, axis, by):
    size = lax.axis_size(axis)
    return lax.ppermute(x, axis, [(i, (i + by) % size) for i in range(size)])


def pair_swap(x, axis):
    size = lax.axis_size(axis)
    return lax.ppermute(x, axis, [(i, i ^ 1) for i in range(size)])


def make_table(bin_count, windows, lag_count):
    lags = jnp.arange(lag_count, dtype=jnp.int32) - lag_count // 2
    bins = jnp.arange(bin_count, dtype=jnp.int32)
    period = 2 * bin_count
    phase = bins[None, :] * ((lags[:, None] + period) % period) % period
    angle = phase.astype(jnp.float32) * (math.pi / bin_count)
    weight = (bin_count * windows) ** (-0.5)
    both = jnp.stack([jnp.cos(angle), -jnp.sin(angle)], axis=1) * weight
    both = both.astype(jnp.bfloat16).reshape(lag_count, 2, bin_count // GROUP, GROUP)
    return both.transpose(0, 2, 1, 3).reshape(lag_count, 2 * bin_count)


def left_side(local, start, rows, lanes):
    tile = lanes.stop - lanes.start
    bin_of_row = lax.broadcasted_iota(jnp.int32, (GROUP, tile), 0)
    bin_of_lane = lax.broadcasted_iota(jnp.int32, (GROUP, tile), 1) // (tile // GROUP)
    same_bin = bin_of_row == bin_of_lane
    re_own, re_other, im_own, im_other = (ref.at[pl.ds(start, rows), :] for ref in local)

    def spread(ref, i):
        return jnp.where(same_bin, jnp.broadcast_to(ref[i : i + 1, lanes], (GROUP, tile)), 0.0)

    pieces = []
    for i in range(rows):
        own = jnp.concatenate([spread(re_own, i), spread(im_own, i)], axis=0)
        other = jnp.concatenate([spread(re_other, i), spread(im_other, i)], axis=0)
        pieces.append(jnp.concatenate([own, other], axis=1).astype(jnp.bfloat16))
    return jnp.concatenate(pieces, axis=0)


def left_sides_kernel(*refs):
    local, out = refs[:4], refs[4]
    channels, depth = local[0].shape
    rows = CHANNEL_BLOCK
    tile = GROUP * 16

    @pl.loop(0, channels // rows)
    def _(b):
        start = pl.multiple_of(b * rows, rows)
        for g in range(depth // tile):
            at = pl.ds(pl.multiple_of(b * rows * 16, rows * 16), rows * 16)
            out[g, at, :] = left_side(local, start, rows, slice(g * tile, (g + 1) * tile))


def left_sides(local):
    channels, depth = local[0].shape
    vmem = pl.BlockSpec(memory_space=pltpu.VMEM)
    return pl.pallas_call(
        left_sides_kernel,
        in_specs=[vmem] * len(local),
        out_specs=vmem,
        out_shape=pltpu.VMEM((depth // (GROUP * 16), channels * 2 * GROUP, 2 * GROUP * 16), jnp.bfloat16),
        compiler_params=pltpu.CompilerParams(vmem_limit_bytes=VMEM),
        cost_estimate=COST,
    )(*local)


def lag_kernel(*refs, first, rounds, local_count, has_total, last):
    table, local, refs = refs[0], refs[1 : 1 + local_count], refs[1 + local_count :]
    partners, refs = refs[: 2 * len(rounds)], refs[2 * len(rounds) :]
    depth = partners[0].shape[0]
    total, refs = (refs[0], refs[1:]) if has_total else (None, refs)
    out, cross = refs[:2] if not last else refs[-4:-2]
    rows = CHANNEL_BLOCK
    width = partners[0].shape[1]
    tile = GROUP * 16
    _, lag_count, channels, _ = out.shape
    mine = pl.ds(pl.multiple_of(lax.axis_index("sub") * lag_count, lag_count), lag_count)
    weights = table[mine, 2 * first : 2 * (first + depth // 16)]
    def block(b, slot):
        start = pl.multiple_of(b * rows, rows)
        for g in range(depth // tile):
            lanes = slice(g * tile, (g + 1) * tile)
            if len(local) == 1:
                left = local[0][g, pl.ds(pl.multiple_of(b * rows * 16, rows * 16), rows * 16), :]
            else:
                left = left_side(local, start, rows, lanes)
            halves = [jnp.concatenate([x[lanes, :] for x in partners[k::2]], axis=1) for k in range(2)]
            right = jnp.concatenate(halves, axis=0)
            part = jnp.dot(left, right, preferred_element_type=jnp.float32).astype(jnp.bfloat16)
            cross[slot, :, g * 2 * GROUP : (g + 1) * 2 * GROUP, :] = part.reshape(rows, 2 * GROUP, part.shape[-1])

        for low in range(0, rows, 8):
            lagged = [jnp.dot(weights, cross[slot, i], preferred_element_type=jnp.float32) for i in range(low, low + 8)]
            at = pl.ds(pl.multiple_of(start + low, 8), 8)
            for n, r in enumerate(rounds):
                stacked = jnp.stack([x[:, n * width : (n + 1) * width] for x in lagged], axis=0)
                tile_out = jnp.swapaxes(stacked, 0, 1)
                if has_total:
                    tile_out = tile_out + total[r, :, at, :]
                if last:
                    stage[b, n, :, low : low + 8, :] = tile_out
                else:
                    out[r, :, at, :] = tile_out

    if last:
        stage, sems = refs[-2:]

        def store(b):
            at = pl.ds(pl.multiple_of(b * rows, rows), rows)
            there = out.at[rounds[0] : rounds[-1] + 1, :, at, :]
            return pltpu.make_async_copy(stage.at[b], there, sems.at[b])

        @pl.loop(0, channels // rows, step=UNROLL)
        def _(b):
            for n in range(UNROLL):
                block(b + n, n)
                store(b + n).start()

        for b in range(channels // rows):
            store(b).wait()
    else:

        @pl.loop(0, channels // rows, step=UNROLL)
        def _(b):
            for n in range(UNROLL):
                block(b + n, n)


def add_lags(table, first, local, partners, total, rounds=(0, 1), last=False, result=None):
    depth, width = partners[0].shape
    channels = local[0].shape[0] if len(local) > 1 else local[0].shape[1] // (2 * GROUP)
    lag_count = table.shape[0] // lax.axis_size("sub")
    block = CHANNEL_BLOCK
    vmem = pl.BlockSpec(memory_space=pltpu.VMEM)
    hbm = pl.BlockSpec(memory_space=pl.ANY)
    operands = [table, *local, *partners]
    in_specs = [vmem] * len(operands)
    aliases = {}
    if total is not None:
        if not last:
            aliases = {len(operands): 0}
        operands.append(total)
        in_specs.append(vmem)
    if result is not None:
        aliases = {len(operands): 0}
        operands.append(result)
        in_specs.append(hbm)
    shape = (ROUNDS, lag_count, channels, width)
    scratch = [pltpu.VMEM((UNROLL, block, depth // 8, len(rounds) * width), jnp.bfloat16)]
    if last:
        blocks = channels // block
        scratch += [
            pltpu.VMEM((blocks, len(rounds), lag_count, block, width), jnp.float32),
            pltpu.SemaphoreType.DMA((blocks,)),
        ]
    return pl.pallas_call(
        functools.partial(lag_kernel, first=first, rounds=rounds, local_count=len(local), has_total=total is not None, last=last),
        in_specs=in_specs,
        out_specs=hbm if last else vmem,
        out_shape=jax.ShapeDtypeStruct(shape, jnp.float32) if last else pltpu.VMEM(shape, jnp.float32),
        input_output_aliases=aliases,
        scratch_shapes=scratch,
        compiler_params=pltpu.CompilerParams(vmem_limit_bytes=VMEM),
        cost_estimate=pl.CostEstimate(
            flops=int(LAG_FLOPS) * len(rounds) // ROUNDS, bytes_accessed=0, transcendentals=0
        ),
    )(*operands)


def bins_first_kernel(x, *outs, sizes, first):
    outs = outs[-len(sizes) :]
    for out, size in zip(outs, sizes):
        if size == x.shape[2] and first:
            first = 0
        for low in range(0, size, 16):
            at = slice(first + low, first + low + 16)
            slabs = [x[s, c, at, :].astype(jnp.float32) for c in range(2) for s in range(x.shape[0])]
            turned = jnp.swapaxes(jnp.stack(slabs, axis=0), 0, 1)
            rows = turned.reshape(16 * len(slabs), x.shape[3]).astype(out.dtype)
            out[low * len(slabs) : (low + 16) * len(slabs), :] = rows
        first += size


def bins_first(x, first, sizes, after):
    windows, parts, bins, channels = x.shape
    read = bins if first else sum(sizes)
    return pl.pallas_call(
        functools.partial(bins_first_kernel, sizes=sizes, first=first),
        grid=(1,),
        in_specs=[pl.BlockSpec((windows, parts, read, channels), lambda b: (0, 0, 0, 0))]
        + [pl.BlockSpec(memory_space=pl.ANY)] * len(after),
        out_specs=[pl.BlockSpec((size * parts * windows, channels), lambda b: (0, 0)) for size in sizes],
        out_shape=[jax.ShapeDtypeStruct((size * parts * windows, channels), x.dtype) for size in sizes],
        compiler_params=pltpu.CompilerParams(vmem_limit_bytes=VMEM),
        cost_estimate=COST,
    )(x, *after)


def channels_first_kernel(own, other, *outs):
    quarter = len(outs) // 4
    for k, ref in enumerate((own, other)):
        first = 0
        for n in range(quarter):
            plain, turned = outs[4 * n + k], outs[4 * n + 2 + k]
            depth = plain.shape[1]
            for low in range(0, depth, 128):
                tile = ref[first + low : first + low + 128, :].astype(jnp.float32).T
                real_lane = lax.broadcasted_iota(jnp.int32, tile.shape, 1) % 16 < 8
                plain[:, low : low + 128] = tile
                swapped = jnp.where(real_lane, -pltpu.roll(tile, 128 - 8, 1), pltpu.roll(tile, 8, 1))
                turned[:, low : low + 128] = swapped
            first += depth


def channels_first(own, other, depths):
    outs = pl.pallas_call(
        channels_first_kernel,
        out_shape=[pltpu.VMEM((own.shape[1], depth), jnp.float32) for depth in depths for _ in range(4)],
        in_specs=[pl.BlockSpec(memory_space=pltpu.VMEM)] * 2,
        out_specs=[pl.BlockSpec(memory_space=pltpu.VMEM)] * (4 * len(depths)),
        compiler_params=pltpu.CompilerParams(vmem_limit_bytes=VMEM),
        cost_estimate=COST,
    )(own, other)
    return [outs[4 * n : 4 * n + 4] for n in range(len(depths))]


def choose_kernel(direction, of_pair, mine, behind, ahead, *rest):
    far, near, held, sems = rest[-4:]
    odd = lax.axis_index("blk") % 2

    def fetch(source, n):
        return pltpu.make_async_copy(source, held.at[n], sems.at[n])

    pl.when(direction[1, 0] == 1)(lambda: fetch(ahead, 0).start())
    pl.when(direction[1, 0] != 1)(lambda: fetch(behind, 0).start())
    pl.when(of_pair[0] == odd)(lambda: fetch(mine, 1).start())
    pl.when((of_pair[0] != odd) & (odd == 1))(lambda: fetch(behind, 1).start())
    pl.when((of_pair[0] != odd) & (odd == 0))(lambda: fetch(ahead, 1).start())
    for n, out in enumerate((far, near)):
        fetch(mine, n).wait()
        pltpu.make_async_copy(held.at[n], out, sems.at[n]).start()
    for n, out in enumerate((far, near)):
        pltpu.make_async_copy(held.at[n], out, sems.at[n]).wait()


def choose(direction, of_pair, mine, behind, ahead, after):
    smem = pl.BlockSpec(memory_space=pltpu.SMEM)
    hbm = pl.BlockSpec(memory_space=pl.ANY)
    return pl.pallas_call(
        choose_kernel,
        in_specs=[smem, smem] + [hbm] * (3 + len(after)),
        out_specs=[hbm, hbm],
        out_shape=[jax.ShapeDtypeStruct(mine.shape, mine.dtype)] * 2,
        scratch_shapes=[pltpu.VMEM((2, *mine.shape), mine.dtype), pltpu.SemaphoreType.DMA((2,))],
        compiler_params=pltpu.CompilerParams(vmem_limit_bytes=VMEM),
        cost_estimate=COST,
    )(direction, of_pair, mine, behind, ahead, *after)


def per_device(spectra, direction):
    windows, _, bin_count, channels = spectra.shape
    with jax.named_scope("direction_of_pair"):
        of_pair = pair_swap(direction[0], "blk")
    table = make_table(bin_count, windows * lax.axis_size("sub"), LAGS)

    mine = bins_first(spectra, 0, CHUNKS[:1], [])
    *later, whole = bins_first(spectra, CHUNKS[0], (*CHUNKS[1:], bin_count), mine)
    mine = [*mine, *later]
    behind, ahead = [], []
    for n, x in enumerate(mine):
        with jax.named_scope(f"two_behind_{n}"):
            behind.append(ring_shift(x, "blk", 2))
        with jax.named_scope(f"two_ahead_{n}"):
            ahead.append(ring_shift(x, "blk", -2))
    with jax.named_scope("my_other_half"):
        other = ring_shift(whole, "sub", 1)
    local = channels_first(whole, other, [size * whole.shape[0] // bin_count for size in CHUNKS])

    totals = [None]
    first = 0
    for n, size in enumerate(CHUNKS):
        after = [totals[AFTER[n] + 1]] if n in AFTER else []
        if n == 0:
            after = [local[0][0], table]
        if n in EXPAND:
            m = EXPAND[n]
            local[m] = [left_sides(local[m])]
            after = after + local[m]
        far_own, passed_on = choose(direction, of_pair, mine[n], behind[n], ahead[n], after)
        if n in NEAR_GATE:
            passed_on, _ = lax.optimization_barrier((passed_on, totals[NEAR_GATE[n] + 1]))
        with jax.named_scope(f"near_{n}"):
            near_own = pair_swap(passed_on, "blk")
        with jax.named_scope(f"far_other_half_{n}"):
            far_other = ring_shift(far_own, "sub", 1)
        ends = n == len(CHUNKS) - 1
        far_total = None
        if ends and SPLIT:
            far_total = add_lags(table, first, local[n], [far_own, far_other], totals[-1], (1,), True)
        if n in GATE:
            done = far_total if ends and SPLIT and GATE_FAR else totals[GATE[n] + 1]
            near_own, _ = lax.optimization_barrier((near_own, done))
        with jax.named_scope(f"near_other_half_{n}"):
            near_other = ring_shift(near_own, "sub", 1)
        if ends and SPLIT:
            total = add_lags(table, first, local[n], [near_own, near_other], totals[-1], (0,), True, far_total)
        else:
            partners = [near_own, near_other, far_own, far_other]
            total = add_lags(table, first, local[n], partners, totals[-1], last=ends)
        totals.append(total)
        first += size
    return totals[-1][:, None]


def solution(mesh):
    return jax.shard_map(
        per_device,
        mesh=mesh,
        in_specs=(P("sub", None, None, ("grp", "blk")), P(None, "blk")),
        out_specs=P(None, ("grp", "blk"), "sub", None, None),
        check_vma=False,
    )
```

```python
import functools
import math

import jax
import jax.numpy as jnp
from jax import lax
from jax.experimental import pallas as pl
from jax.experimental.pallas import tpu as pltpu
from jax.sharding import PartitionSpec as P

LAGS = 64
ROUNDS = 2
GROUP = 8
CHANNEL_BLOCK = 32
UNROLL = 2
CHUNKS = (64, 64, 64, 64)
VMEM = 20 * 2**20
AFTER = {3: 0}
GATE = {3: 2}
LATE = {1: 2, 2: 3}
LAG_FLOPS = 6e9
RUNS = ((0,), (1, 2), (3,))
COST = pl.CostEstimate(flops=0, bytes_accessed=0, transcendentals=0)


def ring_shift(x, axis, by):
    size = lax.axis_size(axis)
    return lax.ppermute(x, axis, [(i, (i + by) % size) for i in range(size)])


def pair_swap(x, axis):
    size = lax.axis_size(axis)
    return lax.ppermute(x, axis, [(i, i ^ 1) for i in range(size)])


def make_table(bin_count, windows, lag_count):
    lags = jnp.arange(lag_count, dtype=jnp.int32) - lag_count // 2
    bins = jnp.arange(bin_count, dtype=jnp.int32)
    period = 2 * bin_count
    phase = bins[None, :] * ((lags[:, None] + period) % period) % period
    angle = phase.astype(jnp.float32) * (math.pi / bin_count)
    weight = (bin_count * windows) ** (-0.5)
    both = jnp.stack([jnp.cos(angle), -jnp.sin(angle)], axis=1) * weight
    both = both.astype(jnp.bfloat16).reshape(lag_count, 2, bin_count // GROUP, GROUP)
    return both.transpose(0, 2, 1, 3).reshape(lag_count, 2 * bin_count)


def left_side(local, start, rows, lanes):
    tile = lanes.stop - lanes.start
    bin_of_row = lax.broadcasted_iota(jnp.int32, (GROUP, tile), 0)
    bin_of_lane = lax.broadcasted_iota(jnp.int32, (GROUP, tile), 1) // (tile // GROUP)
    same_bin = bin_of_row == bin_of_lane
    re_own, re_other, im_own, im_other = (ref.at[pl.ds(start, rows), :] for ref in local)

    def spread(ref, i):
        return jnp.where(same_bin, jnp.broadcast_to(ref[i : i + 1, lanes], (GROUP, tile)), 0.0)

    pieces = []
    for i in range(rows):
        own = jnp.concatenate([spread(re_own, i), spread(im_own, i)], axis=0)
        other = jnp.concatenate([spread(re_other, i), spread(im_other, i)], axis=0)
        pieces.append(jnp.concatenate([own, other], axis=1).astype(jnp.bfloat16))
    return jnp.concatenate(pieces, axis=0)


def lag_kernel(*refs, first, runs, has_total, last):
    table, refs = refs[0], refs[1:]
    locals_, refs = [refs[4 * n : 4 * n + 4] for n in range(runs)], refs[4 * runs :]
    partners, refs = [refs[4 * n : 4 * n + 4] for n in range(runs)], refs[4 * runs :]
    depths = [x[0].shape[0] for x in partners]
    depth = sum(depths)
    total, refs = (refs[0], refs[1:]) if has_total else (None, refs)
    out, cross = refs[:2] if not last else refs[-4:-2]
    rows = CHANNEL_BLOCK
    width = partners[0][0].shape[1]
    tile = GROUP * 16
    _, lag_count, channels, _ = out.shape
    mine = pl.ds(pl.multiple_of(lax.axis_index("sub") * lag_count, lag_count), lag_count)
    weights = table[mine, 2 * first : 2 * (first + depth // 16)]
    def block(b, slot):
        start = pl.multiple_of(b * rows, rows)
        done = 0
        for n in range(runs):
            for g in range(depths[n] // tile):
                lanes = slice(g * tile, (g + 1) * tile)
                left = left_side(locals_[n], start, rows, lanes)
                halves = [jnp.concatenate([x[lanes, :] for x in partners[n][k::2]], axis=1) for k in range(2)]
                right = jnp.concatenate(halves, axis=0)
                part = jnp.dot(left, right, preferred_element_type=jnp.float32).astype(jnp.bfloat16)
                cross[slot, :, done : done + 2 * GROUP, :] = part.reshape(rows, 2 * GROUP, part.shape[-1])
                done += 2 * GROUP

        for low in range(0, rows, 8):
            lagged = [jnp.dot(weights, cross[slot, i], preferred_element_type=jnp.float32) for i in range(low, low + 8)]
            at = pl.ds(pl.multiple_of(start + low, 8), 8)
            for r in range(ROUNDS):
                stacked = jnp.stack([x[:, r * width : (r + 1) * width] for x in lagged], axis=0)
                tile_out = jnp.swapaxes(stacked, 0, 1)
                if has_total:
                    tile_out = tile_out + total[r, :, at, :]
                if last:
                    stage[b, r, :, low : low + 8, :] = tile_out
                else:
                    out[r, :, at, :] = tile_out
            if last:
                store(b, low).start()

    if last:
        stage, sems = refs[-2:]

        def store(b, low):
            at = pl.ds(pl.multiple_of(b * rows + low, 8), 8)
            ready = stage.at[b, :, :, low : low + 8, :]
            return pltpu.make_async_copy(ready, out.at[:, :, at, :], sems.at[b, low // 8])

        @pl.loop(0, channels // rows, step=UNROLL)
        def _(b):
            for n in range(UNROLL):
                block(b + n, n)

        for b in range(channels // rows):
            for low in range(0, rows, 8):
                store(b, low).wait()
    else:

        @pl.loop(0, channels // rows, step=UNROLL)
        def _(b):
            for n in range(UNROLL):
                block(b + n, n)


def add_lags(table, first, locals_, partners, total, last):
    width = partners[0][0].shape[1]
    depth = sum(x[0].shape[0] for x in partners)
    channels = locals_[0][0].shape[0]
    lag_count = table.shape[0] // lax.axis_size("sub")
    block = CHANNEL_BLOCK
    vmem = pl.BlockSpec(memory_space=pltpu.VMEM)
    operands = [table, *(x for run in locals_ for x in run), *(x for run in partners for x in run)]
    aliases = {}
    if total is not None:
        if not last:
            aliases = {len(operands): 0}
        operands.append(total)
    shape = (ROUNDS, lag_count, channels, width)
    scratch = [pltpu.VMEM((UNROLL, block, depth // 8, ROUNDS * width), jnp.bfloat16)]
    if last:
        blocks = channels // block
        scratch += [pltpu.VMEM((blocks, ROUNDS, lag_count, block, width), jnp.float32), pltpu.SemaphoreType.DMA((blocks, block // 8))]
    return pl.pallas_call(
        functools.partial(lag_kernel, first=first, runs=len(partners), has_total=total is not None, last=last),
        in_specs=[vmem] * len(operands),
        out_specs=pl.BlockSpec(memory_space=pl.ANY) if last else vmem,
        out_shape=jax.ShapeDtypeStruct(shape, jnp.float32) if last else pltpu.VMEM(shape, jnp.float32),
        input_output_aliases=aliases,
        scratch_shapes=scratch,
        compiler_params=pltpu.CompilerParams(vmem_limit_bytes=VMEM),
        cost_estimate=pl.CostEstimate(flops=int(LAG_FLOPS) * len(partners), bytes_accessed=0, transcendentals=0),
    )(*operands)


def bins_first_kernel(x, *outs, sizes, first):
    outs = outs[-len(sizes) :]
    for out, size in zip(outs, sizes):
        if size == x.shape[2] and first:
            first = 0
        step = 8 if first % 16 or size % 16 else 16
        for low in range(0, size, step):
            at = slice(first + low, first + low + step)
            slabs = [x[s, c, at, :].astype(jnp.float32) for c in range(2) for s in range(x.shape[0])]
            turned = jnp.swapaxes(jnp.stack(slabs, axis=0), 0, 1)
            rows = turned.reshape(step * len(slabs), x.shape[3]).astype(out.dtype)
            out[low * len(slabs) : (low + step) * len(slabs), :] = rows
        first += size


def bins_first(x, first, sizes, after):
    windows, parts, bins, channels = x.shape
    read = bins if first else sum(sizes)
    return pl.pallas_call(
        functools.partial(bins_first_kernel, sizes=sizes, first=first),
        grid=(1,),
        in_specs=[pl.BlockSpec((windows, parts, read, channels), lambda b: (0, 0, 0, 0))]
        + [pl.BlockSpec(memory_space=pl.ANY)] * len(after),
        out_specs=[pl.BlockSpec((size * parts * windows, channels), lambda b: (0, 0)) for size in sizes],
        out_shape=[jax.ShapeDtypeStruct((size * parts * windows, channels), x.dtype) for size in sizes],
        compiler_params=pltpu.CompilerParams(vmem_limit_bytes=VMEM),
        cost_estimate=COST,
    )(x, *after)


def channels_first_kernel(own, other, *outs):
    quarter = len(outs) // 4
    for k, ref in enumerate((own, other)):
        first = 0
        for n in range(quarter):
            plain, turned = outs[4 * n + k], outs[4 * n + 2 + k]
            depth = plain.shape[1]
            for low in range(0, depth, 128):
                tile = ref[first + low : first + low + 128, :].astype(jnp.float32).T
                real_lane = lax.broadcasted_iota(jnp.int32, tile.shape, 1) % 16 < 8
                plain[:, low : low + 128] = tile
                swapped = jnp.where(real_lane, -pltpu.roll(tile, 128 - 8, 1), pltpu.roll(tile, 8, 1))
                turned[:, low : low + 128] = swapped
            first += depth


def channels_first(own, other, depths):
    outs = pl.pallas_call(
        channels_first_kernel,
        out_shape=[pltpu.VMEM((own.shape[1], depth), jnp.float32) for depth in depths for _ in range(4)],
        in_specs=[pl.BlockSpec(memory_space=pltpu.VMEM)] * 2,
        out_specs=[pl.BlockSpec(memory_space=pltpu.VMEM)] * (4 * len(depths)),
        compiler_params=pltpu.CompilerParams(vmem_limit_bytes=VMEM),
        cost_estimate=COST,
    )(own, other)
    return [outs[4 * n : 4 * n + 4] for n in range(len(depths))]


def choose_kernel(direction, of_pair, mine, behind, ahead, *rest):
    far, near, held, sems = rest[-4:]
    odd = lax.axis_index("blk") % 2

    def fetch(source, n):
        return pltpu.make_async_copy(source, held.at[n], sems.at[n])

    pl.when(direction[1, 0] == 1)(lambda: fetch(ahead, 0).start())
    pl.when(direction[1, 0] != 1)(lambda: fetch(behind, 0).start())
    pl.when(of_pair[0] == odd)(lambda: fetch(mine, 1).start())
    pl.when((of_pair[0] != odd) & (odd == 1))(lambda: fetch(behind, 1).start())
    pl.when((of_pair[0] != odd) & (odd == 0))(lambda: fetch(ahead, 1).start())
    for n, out in enumerate((far, near)):
        fetch(mine, n).wait()
        pltpu.make_async_copy(held.at[n], out, sems.at[n]).start()
    for n, out in enumerate((far, near)):
        pltpu.make_async_copy(held.at[n], out, sems.at[n]).wait()


def choose(direction, of_pair, mine, behind, ahead, after):
    smem = pl.BlockSpec(memory_space=pltpu.SMEM)
    hbm = pl.BlockSpec(memory_space=pl.ANY)
    return pl.pallas_call(
        choose_kernel,
        in_specs=[smem, smem] + [hbm] * (3 + len(after)),
        out_specs=[hbm, hbm],
        out_shape=[jax.ShapeDtypeStruct(mine.shape, mine.dtype)] * 2,
        scratch_shapes=[pltpu.VMEM((2, *mine.shape), mine.dtype), pltpu.SemaphoreType.DMA((2,))],
        compiler_params=pltpu.CompilerParams(vmem_limit_bytes=VMEM),
        cost_estimate=COST,
    )(direction, of_pair, mine, behind, ahead, *after)


def per_device(spectra, direction):
    windows, _, bin_count, channels = spectra.shape
    with jax.named_scope("direction_of_pair"):
        of_pair = pair_swap(direction[0], "blk")
    table = make_table(bin_count, windows * lax.axis_size("sub"), LAGS)

    mine = bins_first(spectra, 0, CHUNKS[:1], [])
    *later, whole = bins_first(spectra, CHUNKS[0], (*CHUNKS[1:], bin_count), mine)
    mine = [*mine, *later]
    behind, ahead = [], []
    for n, x in enumerate(mine):
        with jax.named_scope(f"two_behind_{n}"):
            behind.append(ring_shift(x, "blk", 2))
        with jax.named_scope(f"two_ahead_{n}"):
            ahead.append(ring_shift(x, "blk", -2))
    with jax.named_scope("my_other_half"):
        other = ring_shift(whole, "sub", 1)
    local = channels_first(whole, other, [size * whole.shape[0] // bin_count for size in CHUNKS])

    @functools.cache
    def chosen(n):
        after = [local[0][0], table] if n == 0 else []
        if n in AFTER:
            after = [total_after(AFTER[n])]
        return choose(direction, of_pair, mine[n], behind[n], ahead[n], after)

    @functools.cache
    def near(n):
        with jax.named_scope(f"near_{n}"):
            return pair_swap(chosen(n)[1], "blk")

    @functools.cache
    def partners(n):
        far_own, near_own = chosen(n)[0], near(n)
        with jax.named_scope(f"far_other_half_{n}"):
            far_other = ring_shift(far_own, "sub", 1)
        if n in GATE:
            near_own, _ = lax.optimization_barrier((near_own, total_after(GATE[n])))
        if n in LATE:
            near_own, _ = lax.optimization_barrier((near_own, chosen(LATE[n])[1]))
        with jax.named_scope(f"near_other_half_{n}"):
            near_other = ring_shift(near_own, "sub", 1)
        return [near_own, near_other, far_own, far_other]

    @functools.cache
    def total_after(n):
        at = next(k for k, run in enumerate(RUNS) if n in run)
        run = RUNS[at]
        total = total_after(RUNS[at - 1][-1]) if at else None
        first, last = sum(CHUNKS[: run[0]]), at == len(RUNS) - 1
        return add_lags(table, first, [local[m] for m in run], [partners(m) for m in run], total, last)

    for n in range(len(CHUNKS)):
        result = total_after(n)
    return result[:, None]


def solution(mesh):
    return jax.shard_map(
        per_device,
        mesh=mesh,
        in_specs=(P("sub", None, None, ("grp", "blk")), P(None, "blk")),
        out_specs=P(None, ("grp", "blk"), "sub", None, None),
        check_vma=False,
    )
```

```python
import functools
import math

import jax
import jax.numpy as jnp
from jax import lax
from jax.experimental import pallas as pl
from jax.experimental.pallas import tpu as pltpu
from jax.sharding import PartitionSpec as P

LAGS = 64
ROUNDS = 2
GROUP = 8
CHANNEL_BLOCK = 64
UNROLL = 1
CHUNKS = (64, 64, 64, 64)
VMEM = 20 * 2**20
AFTER = {3: 0}
GATE = {3: 2}
LATE = {1: 2, 2: 3}
LAG_FLOPS = 6e9
RUNS = ((0,), (1, 2), (3,))
COST = pl.CostEstimate(flops=0, bytes_accessed=0, transcendentals=0)


def ring_shift(x, axis, by):
    size = lax.axis_size(axis)
    return lax.ppermute(x, axis, [(i, (i + by) % size) for i in range(size)])


def pair_swap(x, axis):
    size = lax.axis_size(axis)
    return lax.ppermute(x, axis, [(i, i ^ 1) for i in range(size)])


def make_table(bin_count, windows, lag_count):
    lags = jnp.arange(lag_count, dtype=jnp.int32) - lag_count // 2
    bins = jnp.arange(bin_count, dtype=jnp.int32)
    period = 2 * bin_count
    phase = bins[None, :] * ((lags[:, None] + period) % period) % period
    angle = phase.astype(jnp.float32) * (math.pi / bin_count)
    weight = (bin_count * windows) ** (-0.5)
    both = jnp.stack([jnp.cos(angle), -jnp.sin(angle)], axis=1) * weight
    both = both.astype(jnp.bfloat16).reshape(lag_count, 2, bin_count // GROUP, GROUP)
    return both.transpose(0, 2, 1, 3).reshape(lag_count, 2 * bin_count)


def left_side(local, start, rows, lanes):
    tile = lanes.stop - lanes.start
    bin_of_row = lax.broadcasted_iota(jnp.int32, (GROUP, tile), 0)
    bin_of_lane = lax.broadcasted_iota(jnp.int32, (GROUP, tile), 1) // (tile // GROUP)
    same_bin = bin_of_row == bin_of_lane
    re_own, re_other, im_own, im_other = (ref.at[pl.ds(start, rows), :] for ref in local)

    def spread(ref, i):
        return jnp.where(same_bin, jnp.broadcast_to(ref[i : i + 1, lanes], (GROUP, tile)), 0.0)

    pieces = []
    for i in range(rows):
        own = jnp.concatenate([spread(re_own, i), spread(im_own, i)], axis=0)
        other = jnp.concatenate([spread(re_other, i), spread(im_other, i)], axis=0)
        pieces.append(jnp.concatenate([own, other], axis=1).astype(jnp.bfloat16))
    return jnp.concatenate(pieces, axis=0)


def lag_kernel(*refs, first, runs, has_total, last):
    table, refs = refs[0], refs[1:]
    locals_, refs = [refs[4 * n : 4 * n + 4] for n in range(runs)], refs[4 * runs :]
    partners, refs = [refs[4 * n : 4 * n + 4] for n in range(runs)], refs[4 * runs :]
    depths = [x[0].shape[0] for x in partners]
    depth = sum(depths)
    total, refs = (refs[0], refs[1:]) if has_total else (None, refs)
    out, cross = refs[:2] if not last else refs[-4:-2]
    rows = CHANNEL_BLOCK
    width = partners[0][0].shape[1]
    tile = GROUP * 16
    _, lag_count, channels, _ = out.shape
    mine = pl.ds(pl.multiple_of(lax.axis_index("sub") * lag_count, lag_count), lag_count)
    weights = table[mine, 2 * first : 2 * (first + depth // 16)]
    def block(b, slot):
        start = pl.multiple_of(b * rows, rows)
        done = 0
        for n in range(runs):
            for g in range(depths[n] // tile):
                lanes = slice(g * tile, (g + 1) * tile)
                left = left_side(locals_[n], start, rows, lanes)
                halves = [jnp.concatenate([x[lanes, :] for x in partners[n][k::2]], axis=1) for k in range(2)]
                right = jnp.concatenate(halves, axis=0)
                part = jnp.dot(left, right, preferred_element_type=jnp.float32).astype(jnp.bfloat16)
                cross[slot, :, done : done + 2 * GROUP, :] = part.reshape(rows, 2 * GROUP, part.shape[-1])
                done += 2 * GROUP

        for low in range(0, rows, 8):
            lagged = [jnp.dot(weights, cross[slot, i], preferred_element_type=jnp.float32) for i in range(low, low + 8)]
            at = pl.ds(pl.multiple_of(start + low, 8), 8)
            for r in range(ROUNDS):
                stacked = jnp.stack([x[:, r * width : (r + 1) * width] for x in lagged], axis=0)
                tile_out = jnp.swapaxes(stacked, 0, 1)
                if has_total:
                    tile_out = tile_out + total[r, :, at, :]
                if last:
                    stage[b, r, :, low : low + 8, :] = tile_out
                else:
                    out[r, :, at, :] = tile_out
            if last:
                store(b, low).start()

    if last:
        stage, sems = refs[-2:]

        def store(b, low):
            at = pl.ds(pl.multiple_of(b * rows + low, 8), 8)
            ready = stage.at[b, :, :, low : low + 8, :]
            return pltpu.make_async_copy(ready, out.at[:, :, at, :], sems.at[b, low // 8])

        @pl.loop(0, channels // rows, step=UNROLL)
        def _(b):
            for n in range(UNROLL):
                block(b + n, n)

        for b in range(channels // rows):
            for low in range(0, rows, 8):
                store(b, low).wait()
    else:

        @pl.loop(0, channels // rows, step=UNROLL)
        def _(b):
            for n in range(UNROLL):
                block(b + n, n)


def add_lags(table, first, locals_, partners, total, last):
    width = partners[0][0].shape[1]
    depth = sum(x[0].shape[0] for x in partners)
    channels = locals_[0][0].shape[0]
    lag_count = table.shape[0] // lax.axis_size("sub")
    block = CHANNEL_BLOCK
    vmem = pl.BlockSpec(memory_space=pltpu.VMEM)
    operands = [table, *(x for run in locals_ for x in run), *(x for run in partners for x in run)]
    aliases = {}
    if total is not None:
        if not last:
            aliases = {len(operands): 0}
        operands.append(total)
    shape = (ROUNDS, lag_count, channels, width)
    scratch = [pltpu.VMEM((UNROLL, block, depth // 8, ROUNDS * width), jnp.bfloat16)]
    if last:
        blocks = channels // block
        scratch += [pltpu.VMEM((blocks, ROUNDS, lag_count, block, width), jnp.float32), pltpu.SemaphoreType.DMA((blocks, block // 8))]
    return pl.pallas_call(
        functools.partial(lag_kernel, first=first, runs=len(partners), has_total=total is not None, last=last),
        in_specs=[vmem] * len(operands),
        out_specs=pl.BlockSpec(memory_space=pl.ANY) if last else vmem,
        out_shape=jax.ShapeDtypeStruct(shape, jnp.float32) if last else pltpu.VMEM(shape, jnp.float32),
        input_output_aliases=aliases,
        scratch_shapes=scratch,
        compiler_params=pltpu.CompilerParams(vmem_limit_bytes=VMEM),
        cost_estimate=pl.CostEstimate(flops=int(LAG_FLOPS) * len(partners), bytes_accessed=0, transcendentals=0),
    )(*operands)


def bins_first_kernel(x, *outs, sizes, first):
    outs = outs[-len(sizes) :]
    for out, size in zip(outs, sizes):
        if size == x.shape[2] and first:
            first = 0
        step = 8 if first % 16 or size % 16 else 16
        for low in range(0, size, step):
            at = slice(first + low, first + low + step)
            slabs = [x[s, c, at, :].astype(jnp.float32) for c in range(2) for s in range(x.shape[0])]
            turned = jnp.swapaxes(jnp.stack(slabs, axis=0), 0, 1)
            rows = turned.reshape(step * len(slabs), x.shape[3]).astype(out.dtype)
            out[low * len(slabs) : (low + step) * len(slabs), :] = rows
        first += size


def bins_first(x, first, sizes, after):
    windows, parts, bins, channels = x.shape
    read = bins if first else sum(sizes)
    return pl.pallas_call(
        functools.partial(bins_first_kernel, sizes=sizes, first=first),
        grid=(1,),
        in_specs=[pl.BlockSpec((windows, parts, read, channels), lambda b: (0, 0, 0, 0))]
        + [pl.BlockSpec(memory_space=pl.ANY)] * len(after),
        out_specs=[pl.BlockSpec((size * parts * windows, channels), lambda b: (0, 0)) for size in sizes],
        out_shape=[jax.ShapeDtypeStruct((size * parts * windows, channels), x.dtype) for size in sizes],
        compiler_params=pltpu.CompilerParams(vmem_limit_bytes=VMEM),
        cost_estimate=COST,
    )(x, *after)


def channels_first_kernel(own, other, *outs):
    quarter = len(outs) // 4
    for k, ref in enumerate((own, other)):
        first = 0
        for n in range(quarter):
            plain, turned = outs[4 * n + k], outs[4 * n + 2 + k]
            depth = plain.shape[1]
            for low in range(0, depth, 128):
                tile = ref[first + low : first + low + 128, :].astype(jnp.float32).T
                real_lane = lax.broadcasted_iota(jnp.int32, tile.shape, 1) % 16 < 8
                plain[:, low : low + 128] = tile
                swapped = jnp.where(real_lane, -pltpu.roll(tile, 128 - 8, 1), pltpu.roll(tile, 8, 1))
                turned[:, low : low + 128] = swapped
            first += depth


def channels_first(own, other, depths):
    outs = pl.pallas_call(
        channels_first_kernel,
        out_shape=[pltpu.VMEM((own.shape[1], depth), jnp.float32) for depth in depths for _ in range(4)],
        in_specs=[pl.BlockSpec(memory_space=pltpu.VMEM)] * 2,
        out_specs=[pl.BlockSpec(memory_space=pltpu.VMEM)] * (4 * len(depths)),
        compiler_params=pltpu.CompilerParams(vmem_limit_bytes=VMEM),
        cost_estimate=COST,
    )(own, other)
    return [outs[4 * n : 4 * n + 4] for n in range(len(depths))]


def choose_kernel(direction, of_pair, mine, behind, ahead, *rest):
    far, near, held, sems = rest[-4:]
    odd = lax.axis_index("blk") % 2

    half = mine.shape[0] // 2
    pieces = [(n, k) for n in range(2) for k in range(2)]

    def fetch(source, n, k):
        at = slice(k * half, (k + 1) * half)
        return pltpu.make_async_copy(source.at[at, :], held.at[n, at, :], sems.at[n, k])

    def store(n, k):
        at = slice(k * half, (k + 1) * half)
        return pltpu.make_async_copy(held.at[n, at, :], (far, near)[n].at[at, :], sems.at[n, k])

    def fetch_both(source, n):
        for k in range(2):
            fetch(source, n, k).start()

    pl.when(direction[1, 0] == 1)(lambda: fetch_both(ahead, 0))
    pl.when(direction[1, 0] != 1)(lambda: fetch_both(behind, 0))
    pl.when(of_pair[0] == odd)(lambda: fetch_both(mine, 1))
    pl.when((of_pair[0] != odd) & (odd == 1))(lambda: fetch_both(behind, 1))
    pl.when((of_pair[0] != odd) & (odd == 0))(lambda: fetch_both(ahead, 1))
    for n, k in pieces:
        fetch(mine, n, k).wait()
        store(n, k).start()
    for n, k in pieces:
        store(n, k).wait()


def choose(direction, of_pair, mine, behind, ahead, after):
    smem = pl.BlockSpec(memory_space=pltpu.SMEM)
    hbm = pl.BlockSpec(memory_space=pl.ANY)
    return pl.pallas_call(
        choose_kernel,
        in_specs=[smem, smem] + [hbm] * (3 + len(after)),
        out_specs=[hbm, hbm],
        out_shape=[jax.ShapeDtypeStruct(mine.shape, mine.dtype)] * 2,
        scratch_shapes=[pltpu.VMEM((2, *mine.shape), mine.dtype), pltpu.SemaphoreType.DMA((2, 2))],
        compiler_params=pltpu.CompilerParams(vmem_limit_bytes=VMEM),
        cost_estimate=COST,
    )(direction, of_pair, mine, behind, ahead, *after)


def per_device(spectra, direction):
    windows, _, bin_count, channels = spectra.shape
    with jax.named_scope("direction_of_pair"):
        of_pair = pair_swap(direction[0], "blk")
    table = make_table(bin_count, windows * lax.axis_size("sub"), LAGS)

    mine = bins_first(spectra, 0, CHUNKS[:1], [])
    *later, whole = bins_first(spectra, CHUNKS[0], (*CHUNKS[1:], bin_count), mine)
    mine = [*mine, *later]
    behind, ahead = [], []
    for n, x in enumerate(mine):
        with jax.named_scope(f"two_behind_{n}"):
            behind.append(ring_shift(x, "blk", 2))
        with jax.named_scope(f"two_ahead_{n}"):
            ahead.append(ring_shift(x, "blk", -2))
    with jax.named_scope("my_other_half"):
        other = ring_shift(whole, "sub", 1)
    local = channels_first(whole, other, [size * whole.shape[0] // bin_count for size in CHUNKS])

    @functools.cache
    def chosen(n):
        after = [local[0][0], table] if n == 0 else []
        if n in AFTER:
            after = [total_after(AFTER[n])]
        return choose(direction, of_pair, mine[n], behind[n], ahead[n], after)

    @functools.cache
    def near(n):
        with jax.named_scope(f"near_{n}"):
            return pair_swap(chosen(n)[1], "blk")

    @functools.cache
    def partners(n):
        far_own, near_own = chosen(n)[0], near(n)
        with jax.named_scope(f"far_other_half_{n}"):
            far_other = ring_shift(far_own, "sub", 1)
        if n in GATE:
            near_own, _ = lax.optimization_barrier((near_own, total_after(GATE[n])))
        if n in LATE:
            near_own, _ = lax.optimization_barrier((near_own, chosen(LATE[n])[1]))
        with jax.named_scope(f"near_other_half_{n}"):
            near_other = ring_shift(near_own, "sub", 1)
        return [near_own, near_other, far_own, far_other]

    @functools.cache
    def total_after(n):
        at = next(k for k, run in enumerate(RUNS) if n in run)
        run = RUNS[at]
        total = total_after(RUNS[at - 1][-1]) if at else None
        first, last = sum(CHUNKS[: run[0]]), at == len(RUNS) - 1
        return add_lags(table, first, [local[m] for m in run], [partners(m) for m in run], total, last)

    for n in range(len(CHUNKS)):
        result = total_after(n)
    return result[:, None]


def solution(mesh):
    return jax.shard_map(
        per_device,
        mesh=mesh,
        in_specs=(P("sub", None, None, ("grp", "blk")), P(None, "blk")),
        out_specs=P(None, ("grp", "blk"), "sub", None, None),
        check_vma=False,
    )
```
